128 devices in a mesh: grp: 8 (over z, x_hi), shard: 16 (over y, x_lo, core).
Axes of the slice: x: 4 (x_hi: 2, x_lo: 2; x = x_hi * 2 + x_lo), y: 4, z: 4, core: 2. Of those that a mesh axis runs over, the one named last changes fastest.
Arguments:
- points: bfloat16 [262144, 768], P(('grp', 'shard')), may hold values from -6 to 6
- local_ids: int32 [262144], P(('grp', 'shard')), may hold values from 0 to 2047
- block_counts: int32 [128, 128], P(('grp', 'shard')), may hold values from 0 to 16, as said below
- centroids: float32 [262144, 768], P(('grp', 'shard')), may hold values from -6 to 6
- counts: float32 [262144], P(('grp', 'shard')), may hold values from 1 to 8
- queries: bfloat16 [4096, 768], P(('grp', 'shard')), may hold values from -6 to 6
Outputs:
- updated: float32 [262144, 768], P(('grp', 'shard'))
- new_counts: float32 [262144], P(('grp', 'shard'))
- distance: float32 [4096], P(('grp', 'shard'))
The draws below stay inside these ranges and needn't reach their ends.
Inputs may be any that keep to these rules, and one draw needn't show every extreme that they name: block_counts[d, o] counts the occupied slots at the start of owner o's block in device d's buffer; the other slots of the block are padding whose points and ids matter to nothing. Some owner block is full in every device's buffer, and some owner receives full blocks from every device. `local_ids`: an index within the owning device's block of 2048 centroids.
All inputs are finite; a program needn't handle non-finite values.
Results may differ from the reference program's by a relative error of at most 0.0003.
Values may be sent and summed in bfloat16 or wider, within the bound.
A program may use at most 128 MiB of HBM per device.

```python
import math
import jax
import jax.numpy as jnp
from jax import lax

D = 768
K_OWN = 2048
SLOTS_DEV = 2048
OWNERS = 128
CAP = 16
K = 262144
Q_ALL = 4096


def draw_block_counts(key, part):
    keys = jax.random.split(jax.random.fold_in(key, 17), 5)
    base_fill = jax.random.randint(keys[0], (OWNERS, OWNERS), 0, CAP + 1)
    heavy_owner = jax.random.randint(keys[1], (OWNERS,), 0, 8) == 0
    heavy_fill = jax.random.randint(keys[2], (OWNERS, OWNERS), CAP // 2, CAP + 1)
    filled = jnp.where(heavy_owner[None, :], heavy_fill, base_fill)
    column = jnp.arange(OWNERS, dtype=jnp.int32)[None, :]
    full_owner = jax.random.randint(keys[3], (), 0, OWNERS)
    filled = jnp.where(column == full_owner, CAP, filled)
    row_full = jax.random.randint(keys[4], (OWNERS,), 0, OWNERS)
    filled = jnp.where(column == row_full[:, None], CAP, filled)
    return filled.astype(jnp.int32)


def plant(result, own_key, least, top_value):
    dims = result.shape
    spot = [jax.random.randint(jax.random.fold_in(own_key, axis), (), 0, dims[axis]) for axis in range(len(dims))]
    result = result.at[tuple(spot)].set(least)
    longest = dims.index(max(dims))
    spot[longest] = (spot[longest] + 1) % dims[longest]
    return result.at[tuple(spot)].set(top_value)


def levels(own_key, shape, cuts, low, high):
    gain, own = 1.0, jax.random.fold_in(own_key, 6)
    for dim, parts in cuts:
        draws = jnp.exp(jax.random.uniform(jax.random.fold_in(own, dim), (parts,), jnp.float32, low / len(cuts), high / len(cuts)))
        gain = gain * jnp.repeat(draws, shape[dim] // parts).reshape([-1 if axis == dim else 1 for axis in range(len(shape))])
    return gain


def centred(own_key, shape, deviation, reach, cuts=(), kind=jnp.bfloat16):
    result = jax.random.normal(own_key, shape, jnp.float32) * deviation
    if len(cuts) > 0:
        result = levels(own_key, shape, cuts, -0.22, 0.18) * result
    return jnp.clip(result, min=-reach, max=reach).astype(kind)


def setup_inputs(seed: int = 0) -> dict:
    key_of = jax.random.split(jax.random.key(seed), 7)
    points = centred(key_of[0], (OWNERS * SLOTS_DEV, D), 1.0, 6.0, ((0, 128),))
    local_ids = plant(jax.random.randint(key_of[1], (OWNERS * SLOTS_DEV,), 0, K_OWN), jax.random.fold_in(key_of[1], 1), 0, K_OWN - 1).astype(jnp.int32)
    block_counts = draw_block_counts(jax.random.fold_in(key_of[6], 71), 0)
    centroids = centred(key_of[3], (K, D), 1.0, 6.0, ((0, 128),), jnp.float32)
    counts = jnp.clip(jnp.exp(math.log(8.0) - 2.0794415 * jax.random.uniform(key_of[4], (K,), jnp.float32) ** levels(key_of[4], (K,), ((0, 128),), -0.2, 0.2)), 1.0, 8.0)
    queries = centred(key_of[5], (Q_ALL, D), 1.0, 6.0, ((0, 128),))
    return dict(points=points, local_ids=local_ids, block_counts=block_counts, centroids=centroids, counts=counts, queries=queries)


def reference(points, local_ids, block_counts, centroids, counts, queries):
    capacity = SLOTS_DEV // OWNERS
    routed = points.reshape(OWNERS, OWNERS, capacity, D)
    slot_index = jnp.arange(capacity, dtype=jnp.int32)
    occupied = slot_index[None, None, :] < block_counts[:, :, None]
    target = jnp.where(occupied, local_ids.reshape(OWNERS, OWNERS, capacity), K_OWN).astype(jnp.int32)

    def per_owner(owner):
        owner_rows = lax.dynamic_index_in_dim(routed, owner, 1, keepdims=False).reshape(OWNERS * capacity, D)
        owner_ids = lax.dynamic_index_in_dim(target, owner, 1, keepdims=False).reshape(OWNERS * capacity)
        owner_sums = jax.ops.segment_sum(owner_rows.astype(jnp.float32), owner_ids, num_segments=K_OWN + 1)
        owner_hits = jax.ops.segment_sum(jnp.ones((OWNERS * capacity,), jnp.float32), owner_ids, num_segments=K_OWN + 1)
        return owner_sums[:K_OWN], owner_hits[:K_OWN]

    row_sums, hits = lax.map(per_owner, jnp.arange(OWNERS, dtype=jnp.int32))
    row_sums = row_sums.reshape(K, D)
    hits = hits.reshape(K)
    new_counts = counts + hits
    updated = centroids + (row_sums - hits[:, None] * centroids) / new_counts[:, None]
    rounded = updated.astype(jnp.bfloat16)
    query_norm = jnp.sum(jnp.square(queries.astype(jnp.float32)), axis=1)

    def fold_min(running, cent_block):
        inner = lax.dot_general(queries, cent_block, (((1,), (1,)), ((), ())), preferred_element_type=jnp.float32)
        cent_norm = jnp.sum(jnp.square(cent_block.astype(jnp.float32)), axis=1)
        return jnp.minimum(running, jnp.min(cent_norm[None, :] - 2.0 * inner, axis=1)), None

    start_min = jnp.full((Q_ALL,), jnp.inf, jnp.float32)
    running, _ = lax.scan(fold_min, start_min, rounded.reshape(OWNERS, K_OWN, D))
    distance = (running + query_norm) / D
    return updated, new_counts, distance
```

```python
import jax
import jax.numpy as jnp
from jax import lax
from jax.experimental import pallas as pl
from jax.experimental.pallas import tpu as pltpu
from jax.sharding import PartitionSpec as P

MESH = pl.DeviceIdType.MESH
OWNERS = 128
CAP = 16
D = 768
EARLY = 512
LATE = D - EARLY
OWN = 2048
TILE = 256
TILES = OWN // TILE
ROWS = 32
BLOCKS = 16
F32 = jnp.float32
BF16 = jnp.bfloat16


def place():
    group = lax.axis_index("grp")
    shard = lax.axis_index("shard")
    return (group % 2) * 2 + (shard // 2) % 2, shard // 4, group // 2, shard % 2


def device(x, y, z, c):
    return (z * 2 + x // 2, y * 4 + (x % 2) * 2 + c)


def linear(x, y, z, c):
    group, shard = device(x, y, z, c)
    return group * 16 + shard


def nt_dot(a, b):
    return lax.dot_general(a, b, (((1,), (1,)), ((), ())), preferred_element_type=F32)


def drain(ref, sem):
    pltpu.make_async_copy(ref, ref, sem).wait()


def kernel(
    points,
    ids_in,
    fill_in,
    cent_in,
    counts_in,
    query_in,
    out_updated,
    out_counts,
    out_dist,
    early,
    late,
    cent,
    queries,
    near,
    far,
    onehot,
    scores,
    norms,
    weight,
    pull,
    ids_a,
    ids_b,
    ids_c,
    ids,
    mins,
    arrived,
    local_sem,
    out_sem,
    gather_send,
    gather_recv,
    twin_send,
    twin_recv,
    small_send,
    small_recv,
    point_send,
    point_recv,
    min_send,
    min_recv,
):
    x, y, z, c = place()
    me = linear(x, y, z, c)
    group, shard = device(x, y, z, c)
    twin = device(x, y, z, 1 - c)

    def offset(j):
        return ((x + (j // 2) % 4) % 4, (y + (j // 8) % 4) % 4, (z + j // 32) % 4, (c + j) % 2)

    load_cent = pltpu.make_async_copy(cent_in, cent, local_sem.at[0])
    load_early = pltpu.make_async_copy(
        points.at[pl.ds(me * CAP, CAP), pl.ds(0, EARLY)],
        early.at[pl.ds(me * CAP, CAP)],
        local_sem.at[1],
    )
    load_late = pltpu.make_async_copy(
        points.at[pl.ds(me * CAP, CAP), pl.ds(EARLY, LATE)],
        late.at[pl.ds(me * CAP, CAP)],
        local_sem.at[2],
    )
    load_query = [
        pltpu.make_async_copy(
            query_in.at[:, pl.ds(f * 256, 256)], queries.at[f, c, z, y, x], local_sem.at[3 + f]
        )
        for f in range(3)
    ]
    for copy in load_query:
        copy.start()
    load_early.start()
    load_late.start()
    load_cent.start()

    barrier = pltpu.get_barrier_semaphore()
    for j in range(1, OWNERS):
        pl.semaphore_signal(barrier, inc=1, device_id=device(*offset(j)), device_id_type=MESH)

    slot_owner = lax.broadcasted_iota(jnp.int32, (16, 128), 1)
    slot_row = lax.broadcasted_iota(jnp.int32, (16, 128), 0)
    spread = jnp.where(slot_owner // 8 == slot_row, fill_in[...].astype(F32), 0.0).astype(BF16)
    into = (
        lax.broadcasted_iota(jnp.int32, (128, 128), 0) % 8
        == lax.broadcasted_iota(jnp.int32, (128, 128), 1) // 16
    )
    fill = jnp.dot(spread, into.astype(F32).astype(BF16), preferred_element_type=F32)
    tagged = jnp.where((slot_owner % 16).astype(F32) < fill, ids_in[...], -1)
    lane_block = lax.broadcasted_iota(jnp.int32, (1, 128), 1) // 16
    for s in range(16):
        half, part = divmod(s, 8)
        row = jnp.zeros((1, 128), jnp.int32)
        for g in range(8):
            piece = tagged[2 * g + half : 2 * g + half + 1]
            turn = ((g - part) % 8) * 16
            row = jnp.where(lane_block == g, pltpu.roll(piece, turn, 1) if turn else piece, row)
        ids_a[s] = row

    for copy in load_query:
        copy.wait()
    pl.semaphore_wait(barrier, OWNERS - 1)

    def peer(axis, k):
        return (
            (x + (k if axis == 0 else 0)) % 4,
            (y + (k if axis == 1 else 0)) % 4,
            (z + (k if axis == 2 else 0)) % 4,
            c,
        )

    def region(f, phase, at):
        px, py, pz, pc = at
        if phase == 0:
            return queries.at[f, pc, pz, py, px]
        if phase == 1:
            return (
                queries.at[f, pc, pz, py],
                queries.at[f, pc, pz, pl.ds(0, 4), px],
                queries.at[f, pc, pl.ds(0, 4), py, px],
            )[f]
        return (
            queries.at[f, pc, pz],
            queries.at[f, pc, pl.ds(0, 4), pl.ds(0, 4), px],
            queries.at[f, pc, pl.ds(0, 4), py],
        )[f]

    def push(phase):
        for k in (1, 3, 2):
            for f in range(3):
                part = region(f, phase, (x, y, z, c))
                pltpu.make_async_remote_copy(
                    part,
                    part,
                    gather_send,
                    gather_recv.at[f, phase, k - 1],
                    device_id=device(*peer((f + phase) % 3, k)),
                    device_id_type=MESH,
                ).start()

    def arrive(phase, f, k):
        drain(region(f, phase, peer((f + phase) % 3, 4 - k)), gather_recv.at[f, phase, k - 1])

    def to_twin(part):
        pltpu.make_async_remote_copy(
            part, part, twin_send, twin_recv, device_id=twin, device_id_type=MESH
        ).start()

    push(0)

    for k in range(1, 16):
        s = (shard + k) % 16
        pltpu.make_async_remote_copy(
            ids_a.at[s],
            ids_b.at[shard],
            small_send.at[0],
            small_recv.at[0],
            device_id=(group, s),
            device_id_type=MESH,
        ).start()
    ids_b[shard] = ids_a[shard]

    def send_points(first, width, dst, which):
        def step(i, carry):
            to = offset((37 * i) % OWNERS)
            pltpu.make_async_remote_copy(
                points.at[pl.ds(linear(*to) * CAP, CAP), pl.ds(first, width)],
                dst.at[pl.ds(me * CAP, CAP)],
                point_send.at[which],
                point_recv.at[which],
                device_id=device(*to),
                device_id_type=MESH,
            ).start()
            return carry

        lax.fori_loop(1, OWNERS, step, 0)

    send_points(0, EARLY, early, 0)

    drain(ids_b.at[pl.ds(0, 15)], small_recv.at[0])
    for g in range(8):
        for half in range(2):
            row = jnp.zeros((1, 128), jnp.int32)
            for part in range(8):
                piece = ids_b[8 * half + part]
                turn = ((part - g) % 8) * 16
                row = jnp.where(
                    lane_block == part, pltpu.roll(piece, turn, 1) if turn else piece, row
                )
            ids_c[g, half] = row
    for k in range(1, 8):
        g = (group + k) % 8
        pltpu.make_async_remote_copy(
            ids_c.at[g],
            ids.at[group],
            small_send.at[1],
            small_recv.at[1],
            device_id=(g, shard),
            device_id_type=MESH,
        ).start()
    ids[group] = ids_c[group]

    for f in range(3):
        for k in (1, 3, 2):
            arrive(0, f, k)
    push(1)
    for f in range(3):
        for k in (1, 3, 2):
            arrive(1, f, k)
    push(2)
    for f in range(3):
        to_twin(region(f, 2, (x, y, z, c)))
    send_points(EARLY, LATE, late, 1)

    drain(ids.at[pl.ds(0, 7)], small_recv.at[1])
    load_cent.wait()
    load_early.wait()
    load_late.wait()
    drain(early.at[pl.ds(0, (OWNERS - 1) * CAP)], point_recv.at[0])

    def mark(t):
        names = t * TILE + lax.broadcasted_iota(jnp.int32, (TILE, 128), 0)
        total = jnp.zeros((TILE, 128), F32)
        for g in range(8):
            for half in range(2):
                hit = jnp.where(ids[g, half] == names, 1.0, 0.0)
                total = total + hit
                onehot[:, pl.ds((2 * g + half) * 128, 128)] = hit.astype(BF16)
        return total

    def early_tile(t, carry):
        rows = pl.ds(pl.multiple_of(t * TILE, TILE), TILE)
        hits = jnp.sum(mark(t), axis=1, keepdims=True)
        sums = jnp.dot(onehot[...], early[...], preferred_element_type=F32)
        before = jnp.concatenate(
            [
                jnp.transpose(jnp.broadcast_to(counts_in[2 * t + i], (128, 128)))
                for i in range(2)
            ],
            axis=0,
        )
        after = before + hits
        for i in range(2):
            out_counts[2 * t + i] = jnp.transpose(after[i * 128 : (i + 1) * 128])[0:1]
        inverse = 1.0 / after[:, 0:1]
        old = cent[rows, 0:EARLY]
        new = old + (sums - hits * old) * inverse
        cent[rows, 0:EARLY] = new
        rounded = new.astype(BF16).astype(F32)
        near[rows] = (-2.0 * rounded).astype(BF16)
        norms[rows] = jnp.broadcast_to(
            jnp.sum(rounded * rounded, axis=1, keepdims=True), (TILE, 128)
        )
        weight[rows] = jnp.broadcast_to(inverse, (TILE, 128))
        pull[rows] = jnp.broadcast_to(hits, (TILE, 128))
        return carry

    lax.fori_loop(0, TILES, early_tile, 0)
    store_early = pltpu.make_async_copy(
        cent.at[:, pl.ds(0, EARLY)], out_updated.at[:, pl.ds(0, EARLY)], out_sem.at[0]
    )
    store_early.start()

    for k in (1, 3, 2):
        for f in range(3):
            arrive(2, f, k)
            to_twin(region(f, 2, peer((f + 2) % 3, 4 - k)))
    drain(queries.at[:, 1 - c], twin_recv)

    def block_of(b):
        return c ^ (b & 1), (z + (b >> 1)) % 4, (y // 2) ^ (b >> 3)

    def query_part(f, b):
        bc, bz, by = block_of(b)
        return queries[f, bc, bz, pl.ds(by * 2, 2)].reshape(256, 256)

    def early_scores(b, carry):
        block = jnp.concatenate([query_part(0, b), query_part(1, b)], axis=1)
        for t in range(TILES):
            rows = pl.ds(t * TILE, TILE)
            scores[b, rows] = nt_dot(near[rows], block)
        return carry

    lax.fori_loop(0, BLOCKS, early_scores, 0)

    drain(late.at[pl.ds(0, (OWNERS - 1) * CAP)], point_recv.at[1])

    def late_tile(t, carry):
        rows = pl.ds(pl.multiple_of(t * TILE, TILE), TILE)
        mark(t)
        sums = jnp.dot(onehot[...], late[...], preferred_element_type=F32)
        old = cent[rows, EARLY:D]
        new = old + (sums - pull[rows, 0:1] * old) * weight[rows, 0:1]
        cent[rows, EARLY:D] = new
        rounded = new.astype(BF16).astype(F32)
        far[rows] = (-2.0 * rounded).astype(BF16)
        norms[rows] += jnp.broadcast_to(
            jnp.sum(rounded * rounded, axis=1, keepdims=True), (TILE, 128)
        )
        return carry

    lax.fori_loop(0, TILES, late_tile, 0)
    store_late = pltpu.make_async_copy(
        cent.at[:, pl.ds(EARLY, LATE)], out_updated.at[:, pl.ds(EARLY, LATE)], out_sem.at[1]
    )
    store_late.start()

    def late_scores(b, carry):
        block = query_part(2, b)
        least = jnp.full((8, 256), jnp.inf, F32)
        for t in range(TILES):
            rows = pl.ds(t * TILE, TILE)
            norm = norms[rows]
            total = nt_dot(far[rows], block) + scores[b, rows]
            total = total + jnp.concatenate([norm, norm], axis=1)
            least = jnp.minimum(least, jnp.min(total.reshape(TILE // 8, 8, 256), axis=0))
        least = jnp.min(least, axis=0, keepdims=True)
        bc, bz, by = block_of(b)
        for i in range(2):
            mins[(bc * 4 + bz) * 4 + by * 2 + i] = least[:, i * 128 : (i + 1) * 128]
        for i in range(2):
            ty = by * 2 + (y % 2 + i) % 2
            row = (bc * 4 + bz) * 4 + ty
            for j in range(4):
                tx = (x + j) % 4

                def send():
                    pltpu.make_async_remote_copy(
                        mins.at[row],
                        arrived.at[me],
                        min_send,
                        min_recv,
                        device_id=device(tx, ty, bz, bc),
                        device_id_type=MESH,
                    ).start()

                if i == 0 and j == 0:
                    pl.when(b > 0)(send)
                else:
                    send()
        return carry

    lax.fori_loop(0, BLOCKS, late_scores, 0)
    arrived[me] = mins[(c * 4 + z) * 4 + y]

    own = query_in[...].astype(F32)
    own_norm = jnp.broadcast_to(jnp.sum(own * own, axis=1, keepdims=True), (ROWS, 128))
    own_norm = jnp.transpose(jnp.concatenate([own_norm] * 4, axis=0))[0:1]

    drain(arrived.at[pl.ds(0, OWNERS - 1)], min_recv)
    best = arrived[0]
    for s in range(1, OWNERS):
        best = jnp.minimum(best, arrived[s])
    best = pltpu.roll(jnp.broadcast_to(best, (8, 128)), ((4 - x) % 4) * ROWS, 1)[0:1]
    out_dist[...] = (best + own_norm) / D

    for part in (
        queries.at[0],
        queries.at[0, 0, pl.ds(0, 2)],
        queries.at[0, 0, 0],
        queries.at[0, 0, 0, pl.ds(0, 2)],
        queries.at[0, 0, 0, 0],
        queries.at[0, 0, 0, 0, 0],
    ):
        drain(part, gather_send)
    drain(queries.at[:, c], twin_send)
    drain(ids_a.at[pl.ds(0, 15)], small_send.at[0])
    drain(ids_c.at[pl.ds(0, 7)], small_send.at[1])
    drain(early.at[pl.ds(0, (OWNERS - 1) * CAP)], point_send.at[0])
    drain(late.at[pl.ds(0, (OWNERS - 1) * CAP)], point_send.at[1])
    drain(arrived.at[pl.ds(0, OWNERS - 1)], min_send)
    store_early.wait()
    store_late.wait()


def body(points, local_ids, block_counts, centroids, counts, queries):
    whole = pl.BlockSpec(memory_space=pltpu.VMEM)
    far_away = pl.BlockSpec(memory_space=pl.ANY)
    updated, new_counts, distance = pl.pallas_call(
        kernel,
        out_shape=(
            jax.ShapeDtypeStruct((OWN, D), F32),
            jax.ShapeDtypeStruct((16, 1, 128), F32),
            jax.ShapeDtypeStruct((1, 128), F32),
        ),
        in_specs=[far_away, whole, whole, far_away, whole, whole],
        out_specs=(far_away, whole, whole),
        scratch_shapes=[
            pltpu.VMEM((OWN, EARLY), BF16),
            pltpu.VMEM((OWN, LATE), BF16),
            pltpu.VMEM((OWN, D), F32),
            pltpu.VMEM((3, 2, 4, 4, 4, ROWS, 256), BF16),
            pltpu.VMEM((OWN, EARLY), BF16),
            pltpu.VMEM((OWN, LATE), BF16),
            pltpu.VMEM((TILE, OWN), BF16),
            pltpu.VMEM((BLOCKS, OWN, 256), F32),
            pltpu.VMEM((OWN, 128), F32),
            pltpu.VMEM((OWN, 128), F32),
            pltpu.VMEM((OWN, 128), F32),
            pltpu.VMEM((16, 1, 128), jnp.int32),
            pltpu.VMEM((16, 1, 128), jnp.int32),
            pltpu.VMEM((8, 2, 1, 128), jnp.int32),
            pltpu.VMEM((8, 2, 1, 128), jnp.int32),
            pltpu.VMEM((32, 1, 128), F32),
            pltpu.VMEM((OWNERS, 1, 128), F32),
            pltpu.SemaphoreType.DMA((6,)),
            pltpu.SemaphoreType.DMA((2,)),
            pltpu.SemaphoreType.DMA,
            pltpu.SemaphoreType.DMA((3, 3, 3)),
            pltpu.SemaphoreType.DMA,
            pltpu.SemaphoreType.DMA,
            pltpu.SemaphoreType.DMA((2,)),
            pltpu.SemaphoreType.DMA((2,)),
            pltpu.SemaphoreType.DMA((2,)),
            pltpu.SemaphoreType.DMA((2,)),
            pltpu.SemaphoreType.DMA,
            pltpu.SemaphoreType.DMA,
        ],
        compiler_params=pltpu.CompilerParams(
            collective_id=0, has_side_effects=True, vmem_limit_bytes=60 * 2**20
        ),
        cost_estimate=pl.CostEstimate(
            flops=20 * 10**9, bytes_accessed=24 * 10**6, transcendentals=0
        ),
        name="kmeans_step",
    )(
        points,
        local_ids.reshape(16, 128),
        block_counts,
        centroids,
        counts.reshape(16, 1, 128),
        queries,
    )
    return updated, new_counts.reshape(OWN), distance[0, :ROWS]


def solution(mesh):
    rows = P(("grp", "shard"), None)
    flat = P(("grp", "shard"))
    return jax.shard_map(
        body,
        mesh=mesh,
        in_specs=(rows, flat, rows, rows, flat, rows),
        out_specs=(rows, flat, flat),
        check_vma=False,
    )
```

```python
import jax
import jax.numpy as jnp
from jax import lax
from jax.experimental import pallas as pl
from jax.experimental.pallas import tpu as pltpu
from jax.sharding import PartitionSpec as P

MESH = pl.DeviceIdType.MESH
OWNERS = 128
CAP = 16
D = 768
EARLY = 512
LATE = D - EARLY
OWN = 2048
TILE = 512
TILES = OWN // TILE
ROWS = 32
BLOCKS = 4
SPAN = 1024
FIRST_CUT = 32
SECOND_CUT = 64
F32 = jnp.float32
BF16 = jnp.bfloat16


def place():
    group = lax.axis_index("grp")
    shard = lax.axis_index("shard")
    return (group % 2) * 2 + (shard // 2) % 2, shard // 4, group // 2, shard % 2


def device(x, y, z, c):
    return (z * 2 + x // 2, y * 4 + (x % 2) * 2 + c)


def linear(x, y, z, c):
    group, shard = device(x, y, z, c)
    return group * 16 + shard


def nt_dot(a, b):
    return lax.dot_general(a, b, (((1,), (1,)), ((), ())), preferred_element_type=F32)


def drain(ref, sem):
    pltpu.make_async_copy(ref, ref, sem).wait()


def kernel(
    points,
    ids_in,
    fill_in,
    cent_in,
    counts_in,
    query_in,
    cent,
    out_counts,
    out_dist,
    early,
    late,
    queries,
    near,
    far,
    onehot,
    scores,
    norms,
    weight,
    pull,
    ids_a,
    ids_b,
    ids_c,
    ids,
    mins,
    arrived,
    row_mins,
    all_mins,
    local_sem,
    gather_send,
    gather_recv,
    twin_send,
    twin_recv,
    small_send,
    small_recv,
    point_send,
    point_recv,
    min_send,
    min_recv,
):
    x, y, z, c = place()
    me = linear(x, y, z, c)
    group, shard = device(x, y, z, c)
    twin = device(x, y, z, 1 - c)

    def offset(j):
        return ((x + (j // 2) % 4) % 4, (y + (j // 8) % 4) % 4, (z + j // 32) % 4, (c + j) % 2)

    load_cent = pltpu.make_async_copy(cent_in, cent, local_sem.at[0])
    load_early = pltpu.make_async_copy(
        points.at[pl.ds(me * CAP, CAP), pl.ds(0, EARLY)],
        early.at[pl.ds(me * CAP, CAP)],
        local_sem.at[1],
    )
    load_late = pltpu.make_async_copy(
        points.at[pl.ds(me * CAP, CAP), pl.ds(EARLY, LATE)],
        late.at[pl.ds(me * CAP, CAP)],
        local_sem.at[2],
    )
    load_query = [
        pltpu.make_async_copy(
            query_in.at[:, pl.ds(f * 256, 256)], queries.at[f, c, x, z, y], local_sem.at[3 + f]
        )
        for f in range(3)
    ]
    for copy in load_query:
        copy.start()
    load_early.start()
    load_late.start()
    load_cent.start()

    barrier = pltpu.get_barrier_semaphore()
    for j in range(1, OWNERS):
        to = (group ^ (j // 16), shard ^ (j % 16))
        pl.semaphore_signal(barrier, inc=1, device_id=to, device_id_type=MESH)

    slot_owner = lax.broadcasted_iota(jnp.int32, (16, 128), 1)
    slot_row = lax.broadcasted_iota(jnp.int32, (16, 128), 0)
    spread = jnp.where(slot_owner // 8 == slot_row, fill_in[...].astype(F32), 0.0).astype(BF16)
    into = (
        lax.broadcasted_iota(jnp.int32, (128, 128), 0) % 8
        == lax.broadcasted_iota(jnp.int32, (128, 128), 1) // 16
    )
    fill = jnp.dot(spread, into.astype(F32).astype(BF16), preferred_element_type=F32)
    tagged = jnp.where((slot_owner % 16).astype(F32) < fill, ids_in[...], -1)
    lane_block = lax.broadcasted_iota(jnp.int32, (1, 128), 1) // 16
    for s in range(16):
        half, part = divmod(s, 8)
        row = jnp.zeros((1, 128), jnp.int32)
        for g in range(8):
            piece = tagged[2 * g + half : 2 * g + half + 1]
            turn = ((g - part) % 8) * 16
            row = jnp.where(lane_block == g, pltpu.roll(piece, turn, 1) if turn else piece, row)
        ids_a[s] = row

    for copy in load_query:
        copy.wait()
    pl.semaphore_wait(barrier, OWNERS - 1)

    def peer(axis, k):
        return (
            (x + (k if axis == 0 else 0)) % 4,
            (y + (k if axis == 1 else 0)) % 4,
            (z + (k if axis == 2 else 0)) % 4,
            c,
        )

    def region(f, phase, at):
        px, py, pz, pc = at
        if phase == 0:
            return queries.at[f, pc, px, pz, py]
        every = pl.ds(0, 4)
        if phase == 1:
            return (
                queries.at[f, pc, every, pz, py],
                queries.at[f, pc, px, pz],
                queries.at[f, pc, px, every, py],
            )[f]
        return (
            queries.at[f, pc, every, pz],
            queries.at[f, pc, px],
            queries.at[f, pc, every, every, py],
        )[f]

    def push_to(part, f, phase, k, slot):
        pltpu.make_async_remote_copy(
            part,
            part,
            gather_send,
            gather_recv.at[f, phase, slot - 1],
            device_id=device(*peer((f + phase) % 3, k)),
            device_id_type=MESH,
        ).start()

    def push(phase, ways):
        for k in ways:
            for f in range(3):
                push_to(region(f, phase, (x, y, z, c)), f, phase, k, k)

    def from_peer(phase, f, k):
        return region(f, phase, peer((f + phase) % 3, 4 - k))

    def from_peer_rows(f, k, first):
        px, py, pz, pc = peer((f + 2) % 3, 4 - k)
        every, some = pl.ds(0, 4), pl.ds(first, 16)
        return (
            queries.at[f, pc, every, pz, every, some],
            queries.at[f, pc, px, every, every, some],
            queries.at[f, pc, every, every, py, some],
        )[f]

    def arrive(phase, f, k):
        drain(from_peer(phase, f, k), gather_recv.at[f, phase, k - 1])

    def to_twin(part):
        pltpu.make_async_remote_copy(
            part, part, twin_send, twin_recv, device_id=twin, device_id_type=MESH
        ).start()

    push(0, (1, 3, 2))

    for k in range(1, 16):
        s = (shard + k) % 16
        pltpu.make_async_remote_copy(
            ids_a.at[s],
            ids_b.at[shard],
            small_send.at[0],
            small_recv.at[0],
            device_id=(group, s),
            device_id_type=MESH,
        ).start()
    ids_b[shard] = ids_a[shard]

    def send_points(first, width, dst, which, start, stop):
        def step(i, carry):
            to = offset((37 * i) % OWNERS)
            pltpu.make_async_remote_copy(
                points.at[pl.ds(linear(*to) * CAP, CAP), pl.ds(first, width)],
                dst.at[pl.ds(me * CAP, CAP)],
                point_send.at[which],
                point_recv.at[which],
                device_id=device(*to),
                device_id_type=MESH,
            ).start()
            return carry

        lax.fori_loop(start, stop, step, 0)

    send_points(0, EARLY, early, 0, 1, FIRST_CUT)
    for f in range(3):
        for k in (1, 3, 2):
            arrive(0, f, k)
    push(1, (1, 3, 2))
    send_points(0, EARLY, early, 0, FIRST_CUT, SECOND_CUT)
    for f in range(3):
        for k in (1, 3, 2):
            arrive(1, f, k)
    push(2, (1, 3))
    for f in range(3):
        to_twin(region(f, 2, (x, y, z, c)))
    send_points(0, EARLY, early, 0, SECOND_CUT, OWNERS)

    drain(ids_b.at[pl.ds(0, 15)], small_recv.at[0])
    for g in range(8):
        for half in range(2):
            row = jnp.zeros((1, 128), jnp.int32)
            for part in range(8):
                piece = ids_b[8 * half + part]
                turn = ((part - g) % 8) * 16
                row = jnp.where(
                    lane_block == part, pltpu.roll(piece, turn, 1) if turn else piece, row
                )
            ids_c[g, half] = row
    for k in range(1, 8):
        g = (group + k) % 8
        pltpu.make_async_remote_copy(
            ids_c.at[g],
            ids.at[group],
            small_send.at[1],
            small_recv.at[1],
            device_id=(g, shard),
            device_id_type=MESH,
        ).start()
    ids[group] = ids_c[group]

    for k, first in ((1, 0), (3, 16)):
        for f in range(3):
            arrive(2, f, k)
            part = region(f, 2, peer((f + 2) % 3, 4 - k))
            push_to(from_peer_rows(f, k, first), f, 2, k, 2)
            to_twin(part)
    send_points(EARLY, LATE, late, 1, 1, OWNERS)

    drain(ids.at[pl.ds(0, 7)], small_recv.at[1])
    load_cent.wait()
    load_early.wait()
    load_late.wait()
    drain(early.at[pl.ds(0, (OWNERS - 1) * CAP)], point_recv.at[0])

    def mark(t):
        names = t * TILE + lax.broadcasted_iota(jnp.int32, (TILE, 128), 0)
        total = jnp.zeros((TILE, 128), F32)
        for g in range(8):
            for half in range(2):
                hit = jnp.where(ids[g, half] == names, 1.0, 0.0)
                total = total + hit
                onehot[:, pl.ds((2 * g + half) * 128, 128)] = hit.astype(BF16)
        return total

    def early_tile(t, carry):
        rows = pl.ds(pl.multiple_of(t * TILE, TILE), TILE)
        hits = jnp.sum(mark(t), axis=1, keepdims=True)
        sums = jnp.dot(onehot[...], early[...], preferred_element_type=F32)
        before = jnp.concatenate(
            [
                jnp.transpose(jnp.broadcast_to(counts_in[4 * t + i], (128, 128)))
                for i in range(4)
            ],
            axis=0,
        )
        after = before + hits
        for i in range(4):
            out_counts[4 * t + i] = jnp.transpose(after[i * 128 : (i + 1) * 128])[0:1]
        inverse = 1.0 / after[:, 0:1]
        old = cent[rows, 0:EARLY]
        new = old + (sums - hits * old) * inverse
        cent[rows, 0:EARLY] = new
        rounded = new.astype(BF16).astype(F32)
        near[rows] = (-2.0 * rounded).astype(BF16)
        norms[rows] = jnp.broadcast_to(
            jnp.sum(rounded * rounded, axis=1, keepdims=True), (TILE, 128)
        )
        weight[rows] = jnp.broadcast_to(inverse, (TILE, 128))
        pull[rows] = jnp.broadcast_to(hits, (TILE, 128))
        return carry

    lax.fori_loop(0, TILES, early_tile, 0)
    for f in range(3):
        arrive(2, f, 2)
        to_twin(region(f, 2, peer((f + 2) % 3, 2)))

    def query_part(f, bc, pair):
        return queries[f, bc, pl.ds(pair * 2, 2)].reshape(SPAN, 256)

    def early_scores(bc, pair):
        block = jnp.concatenate([query_part(0, bc, pair), query_part(1, bc, pair)], axis=1)
        for t in range(OWN // 512):
            rows = pl.ds(t * 512, 512)
            scores[bc * 2 + pair, rows] = nt_dot(near[rows], block)

    def early_pair(pair, bc):
        early_scores(bc, pair)
        return bc

    lax.fori_loop(0, 2, early_pair, c)
    drain(queries.at[:, 1 - c], twin_recv)
    lax.fori_loop(0, 2, early_pair, 1 - c)

    drain(late.at[pl.ds(0, (OWNERS - 1) * CAP)], point_recv.at[1])

    def late_tile(t, carry):
        rows = pl.ds(pl.multiple_of(t * TILE, TILE), TILE)
        mark(t)
        sums = jnp.dot(onehot[...], late[...], preferred_element_type=F32)
        old = cent[rows, EARLY:D]
        new = old + (sums - pull[rows, 0:1] * old) * weight[rows, 0:1]
        cent[rows, EARLY:D] = new
        rounded = new.astype(BF16).astype(F32)
        far[rows] = (-2.0 * rounded).astype(BF16)
        norms[rows] += jnp.broadcast_to(
            jnp.sum(rounded * rounded, axis=1, keepdims=True), (TILE, 128)
        )
        return carry

    lax.fori_loop(0, TILES, late_tile, 0)
    def late_scores(b, carry):
        bc, pair = c ^ 1 ^ (b & 1), (x // 2) ^ 1 ^ (b >> 1)
        block = query_part(2, bc, pair)
        least = jnp.full((8, SPAN), jnp.inf, F32)
        for t in range(OWN // 256):
            rows = pl.ds(t * 256, 256)
            total = nt_dot(far[rows], block) + scores[bc * 2 + pair, rows]
            total = total + jnp.concatenate([norms[rows]] * (SPAN // 128), axis=1)
            least = jnp.minimum(least, jnp.min(total.reshape(32, 8, SPAN), axis=0))
        least = jnp.min(least, axis=0, keepdims=True)
        for i in range(8):
            mins[bc * 4 + pair * 2 + i // 4, i % 4] = least[:, i * 128 : (i + 1) * 128]
        for i in range(2):
            to = pair * 2 + (x + 1 + i) % 2

            def send():
                pltpu.make_async_remote_copy(
                    mins.at[bc * 4 + to],
                    arrived.at[c * 4 + x],
                    min_send.at[0],
                    min_recv.at[0],
                    device_id=device(to, y, z, bc),
                    device_id_type=MESH,
                ).start()

            if i == 1:
                pl.when(b < BLOCKS - 1)(send)
            else:
                send()
        return carry

    lax.fori_loop(0, BLOCKS, late_scores, 0)
    arrived[c * 4 + x] = mins[c * 4 + x]

    own = query_in[...].astype(F32)
    own_norm = jnp.broadcast_to(jnp.sum(own * own, axis=1, keepdims=True), (ROWS, 128))
    own_norm = jnp.transpose(jnp.concatenate([own_norm] * 4, axis=0))[0:1]

    drain(arrived.at[pl.ds(0, 7)], min_recv.at[0])
    for i in range(4):
        best = arrived[0, i]
        for s in range(1, 8):
            best = jnp.minimum(best, arrived[s, i])
        row_mins[i] = best
    for k in range(1, 16):
        ty, tz = (y + k % 4) % 4, (z + k // 4) % 4
        pltpu.make_async_remote_copy(
            row_mins.at[tz],
            all_mins.at[z * 4 + y],
            min_send.at[1],
            min_recv.at[1],
            device_id=device(x, ty, tz, c),
            device_id_type=MESH,
        ).start()
    all_mins[z * 4 + y] = row_mins[z]
    drain(all_mins.at[pl.ds(0, 15)], min_recv.at[1])
    best = all_mins[0]
    for s in range(1, 16):
        best = jnp.minimum(best, all_mins[s])
    best = pltpu.roll(jnp.broadcast_to(best, (8, 128)), ((4 - y) % 4) * ROWS, 1)[0:1]
    out_dist[...] = (best + own_norm) / D

    for part in (
        queries.at[0],
        queries.at[0, 0, pl.ds(0, 2)],
        queries.at[0, 0, 0],
        queries.at[0, 0, 0, pl.ds(0, 2)],
        queries.at[0, 0, 0, 0],
        queries.at[0, 0, 0, 0, 0],
    ):
        drain(part, gather_send)
    drain(queries.at[:, c], twin_send)
    drain(ids_a.at[pl.ds(0, 15)], small_send.at[0])
    drain(ids_c.at[pl.ds(0, 7)], small_send.at[1])
    drain(early.at[pl.ds(0, (OWNERS - 1) * CAP)], point_send.at[0])
    drain(late.at[pl.ds(0, (OWNERS - 1) * CAP)], point_send.at[1])
    drain(arrived.at[pl.ds(0, 7)], min_send.at[0])
    drain(all_mins.at[pl.ds(0, 15)], min_send.at[1])


def write_out(updated, counts, dist, out_updated, out_counts, out_dist, sems):
    rows = OWN // 8
    copies = [
        pltpu.make_async_copy(
            updated.at[pl.ds(i * rows, rows)], out_updated.at[pl.ds(i * rows, rows)], sems.at[i]
        )
        for i in range(8)
    ]
    for copy in copies:
        copy.start()
    for i in range(16):
        out_counts[i : i + 1, :] = counts[i]
    out_dist[...] = dist[:, 0:ROWS]
    for copy in copies:
        copy.wait()


def body(points, local_ids, block_counts, centroids, counts, queries):
    whole = pl.BlockSpec(memory_space=pltpu.VMEM)
    far_away = pl.BlockSpec(memory_space=pl.ANY)
    dma = pltpu.SemaphoreType.DMA
    updated, new_counts, distance = pl.pallas_call(
        kernel,
        out_shape=(
            pltpu.VMEM((OWN, D), F32),
            pltpu.VMEM((16, 1, 128), F32),
            pltpu.VMEM((1, 128), F32),
        ),
        in_specs=[far_away, whole, whole, far_away, whole, whole],
        out_specs=(whole, whole, whole),
        scratch_shapes=[
            pltpu.VMEM((OWN, EARLY), BF16),
            pltpu.VMEM((OWN, LATE), BF16),
            pltpu.VMEM((3, 2, 4, 4, 4, ROWS, 256), BF16),
            pltpu.VMEM((OWN, EARLY), BF16),
            pltpu.VMEM((OWN, LATE), BF16),
            pltpu.VMEM((TILE, OWN), BF16),
            pltpu.VMEM((BLOCKS, OWN, SPAN), F32),
            pltpu.VMEM((OWN, 128), F32),
            pltpu.VMEM((OWN, 128), F32),
            pltpu.VMEM((OWN, 128), F32),
            pltpu.VMEM((16, 1, 128), jnp.int32),
            pltpu.VMEM((16, 1, 128), jnp.int32),
            pltpu.VMEM((8, 2, 1, 128), jnp.int32),
            pltpu.VMEM((8, 2, 1, 128), jnp.int32),
            pltpu.VMEM((8, 4, 1, 128), F32),
            pltpu.VMEM((8, 4, 1, 128), F32),
            pltpu.VMEM((4, 1, 128), F32),
            pltpu.VMEM((16, 1, 128), F32),
            dma((6,)),
            dma,
            dma((3, 3, 3)),
            dma,
            dma,
            dma((2,)),
            dma((2,)),
            dma((2,)),
            dma((2,)),
            dma((2,)),
            dma((2,)),
        ],
        compiler_params=pltpu.CompilerParams(
            collective_id=0, has_side_effects=True, vmem_limit_bytes=54 * 2**20
        ),
        cost_estimate=pl.CostEstimate(
            flops=20 * 10**9, bytes_accessed=24 * 10**6, transcendentals=0
        ),
        name="kmeans_step",
    )(
        points,
        local_ids.reshape(16, 128),
        block_counts,
        centroids,
        counts.reshape(16, 1, 128),
        queries,
    )
    updated, new_counts, distance = pl.pallas_call(
        write_out,
        out_shape=(
            jax.ShapeDtypeStruct((OWN, D), F32),
            jax.ShapeDtypeStruct((16, 128), F32),
            jax.ShapeDtypeStruct((1, ROWS), F32),
        ),
        in_specs=[whole, whole, whole],
        out_specs=(far_away, whole, whole),
        scratch_shapes=[dma((8,))],
        compiler_params=pltpu.CompilerParams(vmem_limit_bytes=4 * 2**20),
        name="write_out",
    )(updated, new_counts, distance)
    return updated, new_counts.reshape(OWN), distance.reshape(ROWS)


def solution(mesh):
    rows = P(("grp", "shard"), None)
    flat = P(("grp", "shard"))
    return jax.shard_map(
        body,
        mesh=mesh,
        in_specs=(rows, flat, rows, rows, flat, rows),
        out_specs=(rows, flat, flat),
        check_vma=False,
    )
```

```python
import jax
import jax.numpy as jnp
from jax import lax
from jax.experimental import pallas as pl
from jax.experimental.pallas import tpu as pltpu
from jax.sharding import PartitionSpec as P

MESH = pl.DeviceIdType.MESH
OWNERS = 128
CAP = 16
D = 768
EARLY = 512
LATE = D - EARLY
OWN = 2048
TILE = 1024
TILES = OWN // TILE
ROWS = 32
BLOCKS = 4
SPAN = 1024
FIRST_CUT = 48
SECOND_CUT = 80
F32 = jnp.float32
BF16 = jnp.bfloat16


def place():
    group = lax.axis_index("grp")
    shard = lax.axis_index("shard")
    return (group % 2) * 2 + (shard // 2) % 2, shard // 4, group // 2, shard % 2


def device(x, y, z, c):
    return (z * 2 + x // 2, y * 4 + (x % 2) * 2 + c)


def linear(x, y, z, c):
    group, shard = device(x, y, z, c)
    return group * 16 + shard


def nt_dot(a, b):
    return lax.dot_general(a, b, (((1,), (1,)), ((), ())), preferred_element_type=F32)


def drain(ref, sem):
    pltpu.make_async_copy(ref, ref, sem).wait()


def kernel(
    points,
    ids_in,
    fill_in,
    cent_in,
    counts_in,
    query_in,
    cent,
    out_counts,
    out_dist,
    early,
    late,
    queries,
    near,
    onehot,
    scores,
    norms,
    held,
    ids_a,
    ids_b,
    ids_c,
    ids,
    mins,
    arrived,
    row_mins,
    all_mins,
    local_sem,
    gather_send,
    gather_recv,
    twin_send,
    twin_recv,
    small_send,
    small_recv,
    point_send,
    point_recv,
    min_send,
    min_recv,
):
    x, y, z, c = place()
    me = linear(x, y, z, c)
    group, shard = device(x, y, z, c)
    twin = device(x, y, z, 1 - c)

    def offset(j):
        return ((x + (j // 2) % 4) % 4, (y + (j // 8) % 4) % 4, (z + j // 32) % 4, (c + j) % 2)

    load_cent = pltpu.make_async_copy(cent_in, cent, local_sem.at[0])
    load_early = pltpu.make_async_copy(
        points.at[pl.ds(me * CAP, CAP), pl.ds(0, EARLY)],
        early.at[pl.ds(me * CAP, CAP)],
        local_sem.at[1],
    )
    load_late = pltpu.make_async_copy(
        points.at[pl.ds(me * CAP, CAP), pl.ds(EARLY, LATE)],
        late.at[pl.ds(me * CAP, CAP)],
        local_sem.at[2],
    )
    load_query = [
        pltpu.make_async_copy(
            query_in.at[:, pl.ds(f * 256, 256)], queries.at[f, c, x, z, y], local_sem.at[3 + f]
        )
        for f in range(3)
    ]
    for copy in load_query:
        copy.start()
    load_early.start()
    load_late.start()
    load_cent.start()

    barrier = pltpu.get_barrier_semaphore()
    for j in range(1, OWNERS):
        to = (group ^ (j // 16), shard ^ (j % 16))
        pl.semaphore_signal(barrier, inc=1, device_id=to, device_id_type=MESH)

    for copy in load_query:
        copy.wait()
    pl.semaphore_wait(barrier, OWNERS - 1)

    def peer(axis, k):
        return (
            (x + (k if axis == 0 else 0)) % 4,
            (y + (k if axis == 1 else 0)) % 4,
            (z + (k if axis == 2 else 0)) % 4,
            c,
        )

    def region(f, phase, at):
        px, py, pz, pc = at
        if phase == 0:
            return queries.at[f, pc, px, pz, py]
        every = pl.ds(0, 4)
        if phase == 1:
            return (
                queries.at[f, pc, every, pz, py],
                queries.at[f, pc, px, pz],
                queries.at[f, pc, px, every, py],
            )[f]
        return (
            queries.at[f, pc, every, pz],
            queries.at[f, pc, px],
            queries.at[f, pc, every, every, py],
        )[f]

    def push_to(part, f, phase, k, slot):
        pltpu.make_async_remote_copy(
            part,
            part,
            gather_send,
            gather_recv.at[f, phase, slot - 1],
            device_id=device(*peer((f + phase) % 3, k)),
            device_id_type=MESH,
        ).start()

    def push(phase, ways):
        for k in ways:
            for f in range(3):
                push_to(region(f, phase, (x, y, z, c)), f, phase, k, k)

    def from_peer(phase, f, k):
        return region(f, phase, peer((f + phase) % 3, 4 - k))

    def from_peer_rows(f, k, first):
        px, py, pz, pc = peer((f + 2) % 3, 4 - k)
        every, some = pl.ds(0, 4), pl.ds(first, 16)
        return (
            queries.at[f, pc, every, pz, every, some],
            queries.at[f, pc, px, every, every, some],
            queries.at[f, pc, every, every, py, some],
        )[f]

    def arrive(phase, f, k):
        drain(from_peer(phase, f, k), gather_recv.at[f, phase, k - 1])

    def to_twin(part):
        pltpu.make_async_remote_copy(
            part, part, twin_send, twin_recv, device_id=twin, device_id_type=MESH
        ).start()

    push(0, (1, 3, 2))

    def send_points(first, width, dst, which, start, stop):
        def step(i, carry):
            to = offset((37 * i) % OWNERS)
            pltpu.make_async_remote_copy(
                points.at[pl.ds(linear(*to) * CAP, CAP), pl.ds(first, width)],
                dst.at[pl.ds(me * CAP, CAP)],
                point_send.at[which],
                point_recv.at[which],
                device_id=device(*to),
                device_id_type=MESH,
            ).start()
            return carry

        lax.fori_loop(start, stop, step, 0)

    send_points(0, EARLY, early, 0, 1, FIRST_CUT)
    slot_owner = lax.broadcasted_iota(jnp.int32, (16, 128), 1)
    slot_row = lax.broadcasted_iota(jnp.int32, (16, 128), 0)
    spread = jnp.where(slot_owner // 8 == slot_row, fill_in[...].astype(F32), 0.0).astype(BF16)
    into = (
        lax.broadcasted_iota(jnp.int32, (128, 128), 0) % 8
        == lax.broadcasted_iota(jnp.int32, (128, 128), 1) // 16
    )
    fill = jnp.dot(spread, into.astype(F32).astype(BF16), preferred_element_type=F32)
    tagged = jnp.where((slot_owner % 16).astype(F32) < fill, ids_in[...], -1)
    lane_block = lax.broadcasted_iota(jnp.int32, (1, 128), 1) // 16
    for s in range(16):
        half, part = divmod(s, 8)
        row = jnp.zeros((1, 128), jnp.int32)
        for g in range(8):
            piece = tagged[2 * g + half : 2 * g + half + 1]
            turn = ((g - part) % 8) * 16
            row = jnp.where(lane_block == g, pltpu.roll(piece, turn, 1) if turn else piece, row)
        ids_a[s] = row

    for k in range(1, 16):
        s = (shard + k) % 16
        pltpu.make_async_remote_copy(
            ids_a.at[s],
            ids_b.at[shard],
            small_send.at[0],
            small_recv.at[0],
            device_id=(group, s),
            device_id_type=MESH,
        ).start()
    ids_b[shard] = ids_a[shard]

    for f in range(3):
        for k in (1, 3, 2):
            arrive(0, f, k)
    push(1, (1, 3, 2))
    send_points(0, EARLY, early, 0, FIRST_CUT, SECOND_CUT)
    for f in range(3):
        for k in (1, 3, 2):
            arrive(1, f, k)
    push(2, (1, 3))
    for f in range(3):
        to_twin(region(f, 2, (x, y, z, c)))
    send_points(0, EARLY, early, 0, SECOND_CUT, OWNERS)

    drain(ids_b.at[pl.ds(0, 15)], small_recv.at[0])
    for g in range(8):
        for half in range(2):
            row = jnp.zeros((1, 128), jnp.int32)
            for part in range(8):
                piece = ids_b[8 * half + part]
                turn = ((part - g) % 8) * 16
                row = jnp.where(
                    lane_block == part, pltpu.roll(piece, turn, 1) if turn else piece, row
                )
            ids_c[g, half] = row
    for k in range(1, 8):
        g = (group + k) % 8
        pltpu.make_async_remote_copy(
            ids_c.at[g],
            ids.at[group],
            small_send.at[1],
            small_recv.at[1],
            device_id=(g, shard),
            device_id_type=MESH,
        ).start()
    ids[group] = ids_c[group]

    for k, first in ((1, 0), (3, 16)):
        for f in range(3):
            arrive(2, f, k)
            part = region(f, 2, peer((f + 2) % 3, 4 - k))
            push_to(from_peer_rows(f, k, first), f, 2, k, 2)
            to_twin(part)
    send_points(EARLY, LATE, late, 1, 1, OWNERS)

    drain(ids.at[pl.ds(0, 7)], small_recv.at[1])

    def mark(t, carry):
        rows = pl.ds(pl.multiple_of(t * 256, 256), 256)
        names = t * 256 + lax.broadcasted_iota(jnp.int32, (256, 128), 0)
        total = jnp.zeros((256, 128), F32)
        for g in range(8):
            for half in range(2):
                hit = jnp.where(ids[g, half] == names, 1.0, 0.0)
                total = total + hit
                onehot[rows, pl.ds((2 * g + half) * 128, 128)] = hit.astype(BF16)
        hits = jnp.sum(total, axis=1, keepdims=True)
        before = jnp.concatenate(
            [
                jnp.transpose(jnp.broadcast_to(counts_in[2 * t + i], (128, 128)))
                for i in range(2)
            ],
            axis=0,
        )
        after = before + hits
        for i in range(2):
            out_counts[2 * t + i] = jnp.transpose(after[i * 128 : (i + 1) * 128])[0:1]
        first = lax.broadcasted_iota(jnp.int32, (256, 128), 1) < 64
        held[rows] = jnp.where(first, 1.0 / after, hits)
        return carry

    lax.fori_loop(0, OWN // 256, mark, 0)

    load_cent.wait()
    load_early.wait()
    load_late.wait()
    drain(early.at[pl.ds(0, (OWNERS - 1) * CAP)], point_recv.at[0])

    def early_tile(t, carry):
        rows = pl.ds(pl.multiple_of(t * TILE, TILE), TILE)
        sums = jnp.dot(onehot[rows], early[...], preferred_element_type=F32)
        old = cent[rows, 0:EARLY]
        new = old + (sums - held[rows, 64:65] * old) * held[rows, 0:1]
        cent[rows, 0:EARLY] = new
        rounded = new.astype(BF16).astype(F32)
        near[rows] = (-2.0 * rounded).astype(BF16)
        norms[rows] = jnp.broadcast_to(
            jnp.sum(rounded * rounded, axis=1, keepdims=True), (TILE, 128)
        )
        return carry

    lax.fori_loop(0, TILES, early_tile, 0)
    for f in range(3):
        arrive(2, f, 2)
        to_twin(region(f, 2, peer((f + 2) % 3, 2)))

    def query_part(f, bc, pair):
        return queries[f, bc, pl.ds(pair * 2, 2)].reshape(SPAN, 256)

    def early_scores(bc, pair):
        block = jnp.concatenate([query_part(0, bc, pair), query_part(1, bc, pair)], axis=1)
        for t in range(OWN // 512):
            rows = pl.ds(t * 512, 512)
            scores[bc * 2 + pair, rows] = nt_dot(near[rows], block)

    for pair in range(2):
        early_scores(c, pair)
    drain(queries.at[:, 1 - c], twin_recv)
    for pair in range(2):
        early_scores(1 - c, pair)

    drain(late.at[pl.ds(0, (OWNERS - 1) * CAP)], point_recv.at[1])

    def late_tile(t, carry):
        rows = pl.ds(pl.multiple_of(t * TILE, TILE), TILE)
        sums = jnp.dot(onehot[rows], late[...], preferred_element_type=F32)
        old = cent[rows, EARLY:D]
        new = old + (sums - held[rows, 64:65] * old) * held[rows, 0:1]
        cent[rows, EARLY:D] = new
        rounded = new.astype(BF16).astype(F32)
        early[rows, 0:LATE] = (-2.0 * rounded).astype(BF16)
        norms[rows] += jnp.broadcast_to(
            jnp.sum(rounded * rounded, axis=1, keepdims=True), (TILE, 128)
        )
        return carry

    lax.fori_loop(0, TILES, late_tile, 0)
    def late_scores(bc, first, count):
        block = queries[2, bc, pl.ds(first, count)].reshape(count * 512, 256)
        at = (first % 2) * 512 if count == 1 else 0
        least = jnp.full((8, count * 512), jnp.inf, F32)
        for t in range(OWN // 256):
            rows = pl.ds(t * 256, 256)
            before = scores[bc * 2 + first // 2, rows, pl.ds(pl.multiple_of(at, 512), count * 512)]
            total = nt_dot(early[rows, 0:LATE], block) + before
            total = total + jnp.concatenate([norms[rows]] * (count * 4), axis=1)
            least = jnp.minimum(least, jnp.min(total.reshape(32, 8, count * 512), axis=0))
        least = jnp.min(least, axis=0, keepdims=True)
        for i in range(count * 4):
            mins[bc * 4 + first + i // 4, i % 4] = least[:, i * 128 : (i + 1) * 128]

    def send_mins(bc, to):
        pltpu.make_async_remote_copy(
            mins.at[bc * 4 + to],
            arrived.at[c * 4 + x],
            min_send.at[0],
            min_recv.at[0],
            device_id=device(to, y, z, bc),
            device_id_type=MESH,
        ).start()

    def late_pair(b, carry):
        bc, pair = c ^ 1 ^ (b & 1), (x // 2) ^ 1 ^ (b >> 1)
        late_scores(bc, pair * 2, 2)
        for i in range(2):
            send_mins(bc, pair * 2 + i)
        return carry

    lax.fori_loop(0, BLOCKS - 1, late_pair, 0)
    beside = x ^ 1
    late_scores(c, beside, 1)
    send_mins(c, beside)
    late_scores(c, x, 1)
    arrived[c * 4 + x] = mins[c * 4 + x]

    own = query_in[...].astype(F32)
    own_norm = jnp.broadcast_to(jnp.sum(own * own, axis=1, keepdims=True), (ROWS, 128))
    own_norm = jnp.transpose(jnp.concatenate([own_norm] * 4, axis=0))[0:1]

    drain(arrived.at[pl.ds(0, 7)], min_recv.at[0])
    for i in range(4):
        best = arrived[0, i]
        for s in range(1, 8):
            best = jnp.minimum(best, arrived[s, i])
        row_mins[i] = best
    for k in range(1, 16):
        ty, tz = (y + k % 4) % 4, (z + k // 4) % 4
        pltpu.make_async_remote_copy(
            row_mins.at[tz],
            all_mins.at[z * 4 + y],
            min_send.at[1],
            min_recv.at[1],
            device_id=device(x, ty, tz, c),
            device_id_type=MESH,
        ).start()
    all_mins[z * 4 + y] = row_mins[z]
    drain(all_mins.at[pl.ds(0, 15)], min_recv.at[1])
    best = all_mins[0]
    for s in range(1, 16):
        best = jnp.minimum(best, all_mins[s])
    best = pltpu.roll(jnp.broadcast_to(best, (8, 128)), ((4 - y) % 4) * ROWS, 1)[0:1]
    out_dist[...] = (best + own_norm) / D

    for part in (
        queries.at[0],
        queries.at[0, 0, pl.ds(0, 2)],
        queries.at[0, 0, 0],
        queries.at[0, 0, 0, pl.ds(0, 2)],
        queries.at[0, 0, 0, 0],
        queries.at[0, 0, 0, 0, 0],
    ):
        drain(part, gather_send)
    drain(queries.at[:, c], twin_send)
    drain(ids_a.at[pl.ds(0, 15)], small_send.at[0])
    drain(ids_c.at[pl.ds(0, 7)], small_send.at[1])
    drain(early.at[pl.ds(0, (OWNERS - 1) * CAP)], point_send.at[0])
    drain(late.at[pl.ds(0, (OWNERS - 1) * CAP)], point_send.at[1])
    drain(arrived.at[pl.ds(0, 7)], min_send.at[0])
    drain(all_mins.at[pl.ds(0, 15)], min_send.at[1])


def write_out(updated, counts, dist, out_updated, out_counts, out_dist, sems):
    rows = OWN // 8
    copies = [
        pltpu.make_async_copy(
            updated.at[pl.ds(i * rows, rows)], out_updated.at[pl.ds(i * rows, rows)], sems.at[i]
        )
        for i in range(8)
    ]
    for copy in copies:
        copy.start()
    for i in range(16):
        out_counts[i : i + 1, :] = counts[i]
    out_dist[...] = dist[:, 0:ROWS]
    for copy in copies:
        copy.wait()


def body(points, local_ids, block_counts, centroids, counts, queries):
    whole = pl.BlockSpec(memory_space=pltpu.VMEM)
    far_away = pl.BlockSpec(memory_space=pl.ANY)
    dma = pltpu.SemaphoreType.DMA
    updated, new_counts, distance = pl.pallas_call(
        kernel,
        out_shape=(
            pltpu.VMEM((OWN, D), F32),
            pltpu.VMEM((16, 1, 128), F32),
            pltpu.VMEM((1, 128), F32),
        ),
        in_specs=[far_away, whole, whole, far_away, whole, whole],
        out_specs=(whole, whole, whole),
        scratch_shapes=[
            pltpu.VMEM((OWN, EARLY), BF16),
            pltpu.VMEM((OWN, LATE), BF16),
            pltpu.VMEM((3, 2, 4, 4, 4, ROWS, 256), BF16),
            pltpu.VMEM((OWN, EARLY), BF16),
            pltpu.VMEM((OWN, OWN), BF16),
            pltpu.VMEM((BLOCKS, OWN, SPAN), F32),
            pltpu.VMEM((OWN, 128), F32),
            pltpu.VMEM((OWN, 128), F32),
            pltpu.VMEM((16, 1, 128), jnp.int32),
            pltpu.VMEM((16, 1, 128), jnp.int32),
            pltpu.VMEM((8, 2, 1, 128), jnp.int32),
            pltpu.VMEM((8, 2, 1, 128), jnp.int32),
            pltpu.VMEM((8, 4, 1, 128), F32),
            pltpu.VMEM((8, 4, 1, 128), F32),
            pltpu.VMEM((4, 1, 128), F32),
            pltpu.VMEM((16, 1, 128), F32),
            dma((6,)),
            dma,
            dma((3, 3, 3)),
            dma,
            dma,
            dma((2,)),
            dma((2,)),
            dma((2,)),
            dma((2,)),
            dma((2,)),
            dma((2,)),
        ],
        compiler_params=pltpu.CompilerParams(
            collective_id=0, has_side_effects=True, vmem_limit_bytes=58 * 2**20 - 2**18
        ),
        cost_estimate=pl.CostEstimate(
            flops=20 * 10**9, bytes_accessed=24 * 10**6, transcendentals=0
        ),
        name="kmeans_step",
    )(
        points,
        local_ids.reshape(16, 128),
        block_counts,
        centroids,
        counts.reshape(16, 1, 128),
        queries,
    )
    updated, new_counts, distance = pl.pallas_call(
        write_out,
        out_shape=(
            jax.ShapeDtypeStruct((OWN, D), F32),
            jax.ShapeDtypeStruct((16, 128), F32),
            jax.ShapeDtypeStruct((1, ROWS), F32),
        ),
        in_specs=[whole, whole, whole],
        out_specs=(far_away, whole, whole),
        scratch_shapes=[dma((8,))],
        compiler_params=pltpu.CompilerParams(vmem_limit_bytes=4 * 2**20),
        name="write_out",
    )(updated, new_counts, distance)
    return updated, new_counts.reshape(OWN), distance.reshape(ROWS)


def solution(mesh):
    rows = P(("grp", "shard"), None)
    flat = P(("grp", "shard"))
    return jax.shard_map(
        body,
        mesh=mesh,
        in_specs=(rows, flat, rows, rows, flat, rows),
        out_specs=(rows, flat, flat),
        check_vma=False,
    )
```

```python
import jax
import jax.numpy as jnp
from jax import lax
from jax.experimental import pallas as pl
from jax.experimental.pallas import tpu as pltpu
from jax.sharding import PartitionSpec as P

MESH = pl.DeviceIdType.MESH
OWNERS = 128
CAP = 16
D = 768
EARLY = 512
LATE = D - EARLY
OWN = 2048
TILE = 1024
TILES = OWN // TILE
ROWS = 32
BLOCKS = 4
SPAN = 1024
FIRST_CUT = 48
SECOND_CUT = 80
F32 = jnp.float32
BF16 = jnp.bfloat16


def place():
    group = lax.axis_index("grp")
    shard = lax.axis_index("shard")
    return (group % 2) * 2 + (shard // 2) % 2, shard // 4, group // 2, shard % 2


def device(x, y, z, c):
    return (z * 2 + x // 2, y * 4 + (x % 2) * 2 + c)


def linear(x, y, z, c):
    group, shard = device(x, y, z, c)
    return group * 16 + shard


def nt_dot(a, b):
    return lax.dot_general(a, b, (((1,), (1,)), ((), ())), preferred_element_type=F32)


def drain(ref, sem):
    pltpu.make_async_copy(ref, ref, sem).wait()


def kernel(
    points,
    ids_in,
    fill_in,
    cent_in,
    counts_in,
    query_in,
    cent,
    out_counts,
    out_dist,
    early,
    late,
    queries,
    near,
    onehot,
    scores,
    norms,
    held,
    ids_a,
    ids_b,
    ids_c,
    ids,
    mins,
    arrived,
    row_mins,
    all_mins,
    local_sem,
    gather_send,
    gather_recv,
    twin_send,
    twin_recv,
    small_send,
    small_recv,
    point_send,
    point_recv,
    min_send,
    min_recv,
):
    x, y, z, c = place()
    me = linear(x, y, z, c)
    group, shard = device(x, y, z, c)
    twin = device(x, y, z, 1 - c)

    def offset(j):
        return ((x + (j // 2) % 4) % 4, (y + (j // 8) % 4) % 4, (z + j // 32) % 4, (c + j) % 2)

    load_cent = pltpu.make_async_copy(cent_in, cent, local_sem.at[0])
    load_early = pltpu.make_async_copy(
        points.at[pl.ds(me * CAP, CAP), pl.ds(0, EARLY)],
        early.at[pl.ds(me * CAP, CAP)],
        local_sem.at[1],
    )
    load_late = pltpu.make_async_copy(
        points.at[pl.ds(me * CAP, CAP), pl.ds(EARLY, LATE)],
        late.at[pl.ds(me * CAP, CAP)],
        local_sem.at[2],
    )
    load_query = [
        pltpu.make_async_copy(
            query_in.at[:, pl.ds(f * 256, 256)], queries.at[f, c, x, z, y], local_sem.at[3 + f]
        )
        for f in range(3)
    ]
    for copy in load_query:
        copy.start()
    load_early.start()
    load_late.start()
    load_cent.start()

    barrier = pltpu.get_barrier_semaphore()
    for j in range(1, OWNERS):
        to = (group ^ (j // 16), shard ^ (j % 16))
        pl.semaphore_signal(barrier, inc=1, device_id=to, device_id_type=MESH)

    for copy in load_query:
        copy.wait()
    pl.semaphore_wait(barrier, OWNERS - 1)

    def peer(axis, k):
        return (
            (x + (k if axis == 0 else 0)) % 4,
            (y + (k if axis == 1 else 0)) % 4,
            (z + (k if axis == 2 else 0)) % 4,
            c,
        )

    def region(f, phase, at):
        px, py, pz, pc = at
        if phase == 0:
            return queries.at[f, pc, px, pz, py]
        every = pl.ds(0, 4)
        if phase == 1:
            return (
                queries.at[f, pc, every, pz, py],
                queries.at[f, pc, px, pz],
                queries.at[f, pc, px, every, py],
            )[f]
        return (
            queries.at[f, pc, every, pz],
            queries.at[f, pc, px],
            queries.at[f, pc, every, every, py],
        )[f]

    def push_to(part, f, phase, k, slot):
        pltpu.make_async_remote_copy(
            part,
            part,
            gather_send,
            gather_recv.at[f, phase, slot - 1],
            device_id=device(*peer((f + phase) % 3, k)),
            device_id_type=MESH,
        ).start()

    def push(phase, ways):
        for k in ways:
            for f in range(3):
                push_to(region(f, phase, (x, y, z, c)), f, phase, k, k)

    def from_peer(phase, f, k):
        return region(f, phase, peer((f + phase) % 3, 4 - k))

    def from_peer_rows(f, k, first):
        px, py, pz, pc = peer((f + 2) % 3, 4 - k)
        every, some = pl.ds(0, 4), pl.ds(first, 16)
        return (
            queries.at[f, pc, every, pz, every, some],
            queries.at[f, pc, px, every, every, some],
            queries.at[f, pc, every, every, py, some],
        )[f]

    def arrive(phase, f, k):
        drain(from_peer(phase, f, k), gather_recv.at[f, phase, k - 1])

    def to_twin(part):
        pltpu.make_async_remote_copy(
            part, part, twin_send, twin_recv, device_id=twin, device_id_type=MESH
        ).start()

    push(0, (1, 3, 2))

    def send_points(first, width, dst, which, start, stop):
        def step(i, carry):
            to = offset((43 * i) % OWNERS)
            pltpu.make_async_remote_copy(
                points.at[pl.ds(linear(*to) * CAP, CAP), pl.ds(first, width)],
                dst.at[pl.ds(me * CAP, CAP)],
                point_send.at[which],
                point_recv.at[which],
                device_id=device(*to),
                device_id_type=MESH,
            ).start()
            return carry

        lax.fori_loop(start, stop, step, 0)

    send_points(0, EARLY, early, 0, 1, FIRST_CUT)
    slot_owner = lax.broadcasted_iota(jnp.int32, (16, 128), 1)
    slot_row = lax.broadcasted_iota(jnp.int32, (16, 128), 0)
    spread = jnp.where(slot_owner // 8 == slot_row, fill_in[...].astype(F32), 0.0).astype(BF16)
    into = (
        lax.broadcasted_iota(jnp.int32, (128, 128), 0) % 8
        == lax.broadcasted_iota(jnp.int32, (128, 128), 1) // 16
    )
    fill = jnp.dot(spread, into.astype(F32).astype(BF16), preferred_element_type=F32)
    tagged = jnp.where((slot_owner % 16).astype(F32) < fill, ids_in[...], -1)
    lane_block = lax.broadcasted_iota(jnp.int32, (1, 128), 1) // 16
    for s in range(16):
        half, part = divmod(s, 8)
        row = jnp.zeros((1, 128), jnp.int32)
        for g in range(8):
            piece = tagged[2 * g + half : 2 * g + half + 1]
            turn = ((g - part) % 8) * 16
            row = jnp.where(lane_block == g, pltpu.roll(piece, turn, 1) if turn else piece, row)
        ids_a[s] = row

    for k in range(1, 16):
        s = (shard + k) % 16
        pltpu.make_async_remote_copy(
            ids_a.at[s],
            ids_b.at[shard],
            small_send.at[0],
            small_recv.at[0],
            device_id=(group, s),
            device_id_type=MESH,
        ).start()
    ids_b[shard] = ids_a[shard]

    for f in range(3):
        for k in (1, 3, 2):
            arrive(0, f, k)
    push(1, (1, 3, 2))
    send_points(0, EARLY, early, 0, FIRST_CUT, SECOND_CUT)
    for f in range(3):
        for k in (1, 3, 2):
            arrive(1, f, k)
    push(2, (1, 3))
    for f in range(3):
        to_twin(region(f, 2, (x, y, z, c)))
    send_points(0, EARLY, early, 0, SECOND_CUT, OWNERS)

    drain(ids_b.at[pl.ds(0, 15)], small_recv.at[0])
    for g in range(8):
        for half in range(2):
            row = jnp.zeros((1, 128), jnp.int32)
            for part in range(8):
                piece = ids_b[8 * half + part]
                turn = ((part - g) % 8) * 16
                row = jnp.where(
                    lane_block == part, pltpu.roll(piece, turn, 1) if turn else piece, row
                )
            ids_c[g, half] = row
    for k in range(1, 8):
        g = (group + k) % 8
        pltpu.make_async_remote_copy(
            ids_c.at[g],
            ids.at[group],
            small_send.at[1],
            small_recv.at[1],
            device_id=(g, shard),
            device_id_type=MESH,
        ).start()
    ids[group] = ids_c[group]

    for k, first in ((1, 0), (3, 16)):
        for f in range(3):
            arrive(2, f, k)
            part = region(f, 2, peer((f + 2) % 3, 4 - k))
            push_to(from_peer_rows(f, k, first), f, 2, k, 2)
            to_twin(part)
    send_points(EARLY, LATE, late, 1, 1, OWNERS)

    drain(ids.at[pl.ds(0, 7)], small_recv.at[1])

    def mark(t, carry):
        rows = pl.ds(pl.multiple_of(t * 256, 256), 256)
        names = t * 256 + lax.broadcasted_iota(jnp.int32, (256, 128), 0)
        total = jnp.zeros((256, 128), F32)
        for g in range(8):
            for half in range(2):
                hit = jnp.where(ids[g, half] == names, 1.0, 0.0)
                total = total + hit
                onehot[rows, pl.ds((2 * g + half) * 128, 128)] = hit.astype(BF16)
        hits = jnp.sum(total, axis=1, keepdims=True)
        before = jnp.concatenate(
            [
                jnp.transpose(jnp.broadcast_to(counts_in[2 * t + i], (128, 128)))
                for i in range(2)
            ],
            axis=0,
        )
        after = before + hits
        for i in range(2):
            out_counts[2 * t + i] = jnp.transpose(after[i * 128 : (i + 1) * 128])[0:1]
        first = lax.broadcasted_iota(jnp.int32, (256, 128), 1) < 64
        held[rows] = jnp.where(first, 1.0 / after, hits)
        return carry

    lax.fori_loop(0, OWN // 256, mark, 0)

    load_cent.wait()
    load_early.wait()
    load_late.wait()
    drain(early.at[pl.ds(0, (OWNERS - 1) * CAP)], point_recv.at[0])

    def early_tile(t, carry):
        rows = pl.ds(pl.multiple_of(t * TILE, TILE), TILE)
        sums = jnp.dot(onehot[rows], early[...], preferred_element_type=F32)
        old = cent[rows, 0:EARLY]
        new = old + (sums - held[rows, 64:65] * old) * held[rows, 0:1]
        cent[rows, 0:EARLY] = new
        rounded = new.astype(BF16).astype(F32)
        near[rows] = (-2.0 * rounded).astype(BF16)
        norms[rows] = jnp.broadcast_to(
            jnp.sum(rounded * rounded, axis=1, keepdims=True), (TILE, 128)
        )
        return carry

    lax.fori_loop(0, TILES, early_tile, 0)
    for f in range(3):
        arrive(2, f, 2)
        to_twin(region(f, 2, peer((f + 2) % 3, 2)))

    def query_part(f, bc, pair):
        return queries[f, bc, pl.ds(pair * 2, 2)].reshape(SPAN, 256)

    def early_scores(bc, pair):
        block = jnp.concatenate([query_part(0, bc, pair), query_part(1, bc, pair)], axis=1)
        for t in range(OWN // 512):
            rows = pl.ds(t * 512, 512)
            scores[bc * 2 + pair, rows] = nt_dot(near[rows], block)

    for pair in range(2):
        early_scores(c, pair)
    drain(queries.at[:, 1 - c], twin_recv)
    for pair in range(2):
        early_scores(1 - c, pair)

    drain(late.at[pl.ds(0, (OWNERS - 1) * CAP)], point_recv.at[1])

    def late_tile(t, carry):
        rows = pl.ds(pl.multiple_of(t * TILE, TILE), TILE)
        sums = jnp.dot(onehot[rows], late[...], preferred_element_type=F32)
        old = cent[rows, EARLY:D]
        new = old + (sums - held[rows, 64:65] * old) * held[rows, 0:1]
        cent[rows, EARLY:D] = new
        rounded = new.astype(BF16).astype(F32)
        early[rows, 0:LATE] = (-2.0 * rounded).astype(BF16)
        norms[rows] += jnp.broadcast_to(
            jnp.sum(rounded * rounded, axis=1, keepdims=True), (TILE, 128)
        )
        return carry

    lax.fori_loop(0, TILES, late_tile, 0)
    def late_scores(bc, first, count):
        block = queries[2, bc, pl.ds(first, count)].reshape(count * 512, 256)
        at = (first % 2) * 512 if count == 1 else 0
        least = jnp.full((8, count * 512), jnp.inf, F32)
        for t in range(OWN // 256):
            rows = pl.ds(t * 256, 256)
            before = scores[bc * 2 + first // 2, rows, pl.ds(pl.multiple_of(at, 512), count * 512)]
            total = nt_dot(early[rows, 0:LATE], block) + before
            total = total + jnp.concatenate([norms[rows]] * (count * 4), axis=1)
            least = jnp.minimum(least, jnp.min(total.reshape(32, 8, count * 512), axis=0))
        least = jnp.min(least, axis=0, keepdims=True)
        for i in range(count * 4):
            mins[bc * 4 + first + i // 4, i % 4] = least[:, i * 128 : (i + 1) * 128]

    def send_mins(bc, to):
        pltpu.make_async_remote_copy(
            mins.at[bc * 4 + to],
            arrived.at[c * 4 + x],
            min_send.at[0],
            min_recv.at[0],
            device_id=device(to, y, z, bc),
            device_id_type=MESH,
        ).start()

    def late_pair(b, carry):
        bc, pair = c ^ 1 ^ (b & 1), (x // 2) ^ 1 ^ (b >> 1)
        late_scores(bc, pair * 2, 2)
        for i in range(2):
            send_mins(bc, pair * 2 + i)
        return carry

    lax.fori_loop(0, BLOCKS - 1, late_pair, 0)
    beside = x ^ 1
    late_scores(c, beside, 1)
    send_mins(c, beside)
    late_scores(c, x, 1)
    arrived[c * 4 + x] = mins[c * 4 + x]

    own = query_in[...].astype(F32)
    own_norm = jnp.broadcast_to(jnp.sum(own * own, axis=1, keepdims=True), (ROWS, 128))
    own_norm = jnp.transpose(jnp.concatenate([own_norm] * 4, axis=0))[0:1]

    drain(arrived.at[pl.ds(0, 7)], min_recv.at[0])
    for i in range(4):
        best = arrived[0, i]
        for s in range(1, 8):
            best = jnp.minimum(best, arrived[s, i])
        row_mins[i] = best
    for k in range(1, 16):
        ty, tz = (y + k % 4) % 4, (z + k // 4) % 4
        pltpu.make_async_remote_copy(
            row_mins.at[tz],
            all_mins.at[z * 4 + y],
            min_send.at[1],
            min_recv.at[1],
            device_id=device(x, ty, tz, c),
            device_id_type=MESH,
        ).start()
    all_mins[z * 4 + y] = row_mins[z]
    drain(all_mins.at[pl.ds(0, 15)], min_recv.at[1])
    best = all_mins[0]
    for s in range(1, 16):
        best = jnp.minimum(best, all_mins[s])
    best = pltpu.roll(jnp.broadcast_to(best, (8, 128)), ((4 - y) % 4) * ROWS, 1)[0:1]
    out_dist[...] = (best + own_norm) / D

    for part in (
        queries.at[0],
        queries.at[0, 0, pl.ds(0, 2)],
        queries.at[0, 0, 0],
        queries.at[0, 0, 0, pl.ds(0, 2)],
        queries.at[0, 0, 0, 0],
        queries.at[0, 0, 0, 0, 0],
    ):
        drain(part, gather_send)
    drain(queries.at[:, c], twin_send)
    drain(ids_a.at[pl.ds(0, 15)], small_send.at[0])
    drain(ids_c.at[pl.ds(0, 7)], small_send.at[1])
    drain(early.at[pl.ds(0, (OWNERS - 1) * CAP)], point_send.at[0])
    drain(late.at[pl.ds(0, (OWNERS - 1) * CAP)], point_send.at[1])
    drain(arrived.at[pl.ds(0, 7)], min_send.at[0])
    drain(all_mins.at[pl.ds(0, 15)], min_send.at[1])


def write_out(updated, counts, dist, out_updated, out_counts, out_dist, sems):
    rows = OWN // 8
    copies = [
        pltpu.make_async_copy(
            updated.at[pl.ds(i * rows, rows)], out_updated.at[pl.ds(i * rows, rows)], sems.at[i]
        )
        for i in range(8)
    ]
    for copy in copies:
        copy.start()
    for i in range(16):
        out_counts[i : i + 1, :] = counts[i]
    out_dist[...] = dist[:, 0:ROWS]
    for copy in copies:
        copy.wait()


def body(points, local_ids, block_counts, centroids, counts, queries):
    whole = pl.BlockSpec(memory_space=pltpu.VMEM)
    far_away = pl.BlockSpec(memory_space=pl.ANY)
    dma = pltpu.SemaphoreType.DMA
    updated, new_counts, distance = pl.pallas_call(
        kernel,
        out_shape=(
            pltpu.VMEM((OWN, D), F32),
            pltpu.VMEM((16, 1, 128), F32),
            pltpu.VMEM((1, 128), F32),
        ),
        in_specs=[far_away, whole, whole, far_away, whole, whole],
        out_specs=(whole, whole, whole),
        scratch_shapes=[
            pltpu.VMEM((OWN, EARLY), BF16),
            pltpu.VMEM((OWN, LATE), BF16),
            pltpu.VMEM((3, 2, 4, 4, 4, ROWS, 256), BF16),
            pltpu.VMEM((OWN, EARLY), BF16),
            pltpu.VMEM((OWN, OWN), BF16),
            pltpu.VMEM((BLOCKS, OWN, SPAN), F32),
            pltpu.VMEM((OWN, 128), F32),
            pltpu.VMEM((OWN, 128), F32),
            pltpu.VMEM((16, 1, 128), jnp.int32),
            pltpu.VMEM((16, 1, 128), jnp.int32),
            pltpu.VMEM((8, 2, 1, 128), jnp.int32),
            pltpu.VMEM((8, 2, 1, 128), jnp.int32),
            pltpu.VMEM((8, 4, 1, 128), F32),
            pltpu.VMEM((8, 4, 1, 128), F32),
            pltpu.VMEM((4, 1, 128), F32),
            pltpu.VMEM((16, 1, 128), F32),
            dma((6,)),
            dma,
            dma((3, 3, 3)),
            dma,
            dma,
            dma((2,)),
            dma((2,)),
            dma((2,)),
            dma((2,)),
            dma((2,)),
            dma((2,)),
        ],
        compiler_params=pltpu.CompilerParams(
            collective_id=0, has_side_effects=True, vmem_limit_bytes=58 * 2**20 - 2**18
        ),
        cost_estimate=pl.CostEstimate(
            flops=20 * 10**9, bytes_accessed=24 * 10**6, transcendentals=0
        ),
        name="kmeans_step",
    )(
        points,
        local_ids.reshape(16, 128),
        block_counts,
        centroids,
        counts.reshape(16, 1, 128),
        queries,
    )
    updated, new_counts, distance = pl.pallas_call(
        write_out,
        out_shape=(
            jax.ShapeDtypeStruct((OWN, D), F32),
            jax.ShapeDtypeStruct((16, 128), F32),
            jax.ShapeDtypeStruct((1, ROWS), F32),
        ),
        in_specs=[whole, whole, whole],
        out_specs=(far_away, whole, whole),
        scratch_shapes=[dma((8,))],
        compiler_params=pltpu.CompilerParams(vmem_limit_bytes=4 * 2**20),
        name="write_out",
    )(updated, new_counts, distance)
    return updated, new_counts.reshape(OWN), distance.reshape(ROWS)


def solution(mesh):
    rows = P(("grp", "shard"), None)
    flat = P(("grp", "shard"))
    return jax.shard_map(
        body,
        mesh=mesh,
        in_specs=(rows, flat, rows, rows, flat, rows),
        out_specs=(rows, flat, flat),
        check_vma=False,
    )
```
